256 devices in a mesh: shots: 16 (over z, core), gy: 4 (over y), gx: 4 (over x).
Axes of the slice: x: 4, y: 4, z: 8, core: 2. Of those that a mesh axis runs over, the one named last changes fastest.
Arguments:
- shot_cells: int32 [16, 4, 4, 16, 4096], P('shots', 'gy', 'gx'), may hold values from 0 to 8191
- shot_dose: float32 [16, 4, 4, 16, 4096], P('shots', 'gy', 'gx'), may hold values from 0.04 to 0.12
- shot_counts: int32 [16, 4, 4, 16], P('shots', 'gy', 'gx'), may hold values from 2048 to 4096, as said below
- materials: int32 [1024, 2048], P(('shots', 'gy'), 'gx'), may hold values from 0 to 3
- coefficients: float32 [4], replicated, may hold values from 0.04 to 0.24
- target: float32 [1024, 2048], P(('shots', 'gy'), 'gx'), may hold values from -6 to 6
Outputs:
- exposure: float32 [1024, 2048], P(('shots', 'gy'), 'gx')
- shot_grad: float32 [16, 4, 4, 16, 4096], P('shots', 'gy', 'gx')
The draws below stay inside these ranges and needn't reach their ends.
Inputs may be any that keep to these rules, and one draw needn't show every extreme that they name: `shot_counts`: in every partition and tile some strip has all 4096 slots live; every count is at least 2048.
All inputs are finite; a program needn't handle non-finite values.
Results may differ from the reference program's by a relative error of at most 0.00007.
Values sent between devices are 32-bit elements; how exact they have to be, the bound alone decides.
No kernel may reach another device: no remote copies, remote signals or barrier semaphores. Data moves between devices by JAX's collectives and lax.ppermute only.
A program may use at most 64 MiB of HBM per device.

```python
import math
import jax
import jax.numpy as jnp

R = 16
CX = 512
SLOTS = 4096
STEPS = 3
MATS = 4
NY = 1024
NX = 2048
N_SHOTS = 16
N_GY = 4
N_GX = 4


def draw_shot_counts(key, part):
    key = jax.random.fold_in(key, 7)
    first, second = jax.random.split(key)
    shape = (N_SHOTS, N_GY, N_GX, N_SHOTS)
    counts = jax.random.randint(first, shape, SLOTS // 2, SLOTS + 1)
    chosen = jax.random.randint(second, (N_SHOTS, N_GY, N_GX, 1), 0, N_SHOTS)
    places = jnp.arange(N_SHOTS, dtype=jnp.int32)[None, None, None, :]
    counts = jnp.where(places == chosen, SLOTS, counts)
    return counts.astype(jnp.int32)


def touch_ends(values, rng, least, largest):
    longest = values.shape.index(max(values.shape))
    spots = []
    for shift in (0, 1):
        where = [jax.random.randint(jax.random.fold_in(rng, axis), (), 0, length) for axis, length in enumerate(values.shape)]
        where[longest] = (where[longest] + shift) % values.shape[longest]
        spots.append(tuple(where))
    return values.at[spots[0]].set(least).at[spots[1]].set(largest)


def level_of(own_key, shape, pieces, smallest, largest):
    def one(dim, blocks):
        heights = jax.random.uniform(jax.random.fold_in(jax.random.fold_in(own_key, 6), dim), (blocks,), jnp.float32, smallest / len(pieces), largest / len(pieces))
        return jnp.repeat(jnp.exp(heights), shape[dim] // blocks).reshape((-1,) + (1,) * (len(shape) - dim - 1))

    factor_of = one(*pieces[0])
    for cut in pieces[1:]:
        factor_of = factor_of * one(*cut)
    return factor_of


def bell_draw(key, dims, scale, limit, cuts=(), held_as=jnp.bfloat16):
    array = jax.random.normal(key, dims, jnp.float32) * scale
    if len(cuts) > 0:
        array = level_of(key, dims, cuts, -0.22, 0.18) * array
    return jnp.clip(array, min=-limit, max=limit).astype(held_as)


def setup_inputs(seed: int = 0) -> dict:
    arg_keys = jax.random.split(jax.random.key(seed), 7)
    return {
        "shot_cells": touch_ends(jax.random.randint(arg_keys[0], (N_SHOTS, N_GY, N_GX, N_SHOTS, SLOTS), 0, R * CX), jax.random.fold_in(arg_keys[0], 1), 0, (R * CX) - 1).astype(jnp.int32),
        "shot_dose": jnp.clip(0.04 + 0.08 * jax.random.uniform(arg_keys[1], (N_SHOTS, N_GY, N_GX, N_SHOTS, SLOTS), jnp.float32) ** level_of(arg_keys[1], (N_SHOTS, N_GY, N_GX, N_SHOTS, SLOTS), ((0, 16), (1, 4), (2, 4)), -0.2, 0.2), 0.04, 0.12),
        "shot_counts": draw_shot_counts(jax.random.fold_in(arg_keys[6], 71), 0),
        "materials": touch_ends(jax.random.randint(arg_keys[3], (NY, NX), 0, MATS), jax.random.fold_in(arg_keys[3], 1), 0, MATS - 1).astype(jnp.int32),
        "coefficients": jnp.clip(jnp.exp(jax.random.uniform(arg_keys[4], (MATS,), jnp.float32, math.log(0.04), math.log(0.24))), 0.04, 0.24),
        "target": bell_draw(arg_keys[5], (NY, NX), 1.0, 6.0, ((0, 64), (1, 4)), jnp.float32),
    }


def neighbours(field):
    padded = jnp.pad(field, 1)
    return padded[2:, 1:-1] + padded[:-2, 1:-1] + padded[1:-1, 2:] + padded[1:-1, :-2]


def reference(shot_cells, shot_dose, shot_counts, materials, coefficients, target):
    parts, tiles_y, tiles_x, owners, slots = shot_cells.shape
    width = materials.shape[1]
    height = materials.shape[0]
    live = jnp.arange(slots, dtype=jnp.int32)[None, None, None, None, :] < shot_counts[..., None]
    dose = jnp.where(live, shot_dose.astype(jnp.float32), jnp.float32(0.0))
    row_in = shot_cells // CX
    col_in = shot_cells % CX
    owner_ids = jnp.arange(owners, dtype=jnp.int32)[None, None, None, :, None]
    tile_y = jnp.arange(tiles_y, dtype=jnp.int32)[None, :, None, None, None]
    tile_x = jnp.arange(tiles_x, dtype=jnp.int32)[None, None, :, None, None]
    grow = owner_ids * (tiles_y * R) + tile_y * R + row_in
    gcol = tile_x * CX + col_in
    flat_index = (grow * width + gcol).astype(jnp.int32)
    dose_grid = jax.ops.segment_sum(dose.reshape(-1), flat_index.reshape(-1), num_segments=height * width)
    dose_grid = dose_grid.reshape(height, width)
    spread = coefficients[materials]
    field = dose_grid
    for step in range(STEPS):
        field = field + spread * (neighbours(field) - 4.0 * field)
    exposure = field
    back = exposure - target
    for step in range(STEPS):
        weighted = spread * back
        back = back + neighbours(weighted) - 4.0 * weighted
    picked = jnp.take(back.reshape(-1), flat_index.reshape(-1)).reshape(shot_cells.shape)
    shot_grad = jnp.where(live, picked, jnp.float32(0.0))
    return exposure, shot_grad
```

```python
import functools

import jax
import jax.numpy as jnp
from jax import lax
from jax.experimental import pallas as pl
from jax.experimental.pallas import tpu as pltpu
from jax.sharding import PartitionSpec as P

STEPS = 3
SPAN = 512
LANES = 128
VMEM = pl.BlockSpec(memory_space=pltpu.VMEM)
SMEM = pl.BlockSpec(memory_space=pltpu.SMEM)
PARAMS = pltpu.CompilerParams(vmem_limit_bytes=32 << 20)
F32 = jnp.float32
BF16 = jnp.bfloat16


def f32(*shape):
    return jax.ShapeDtypeStruct(shape, F32)


def rows_of(value, kind):
    return jnp.broadcast_to(value, (16, value.shape[1])).astype(kind)


def hot(index, groups, filled):
    width = index.shape[1]
    ids = rows_of(index, jnp.int16)
    iota = lax.broadcasted_iota(jnp.int16, (16, width), 0)
    masks = [ids == iota + jnp.int16(16 * g) for g in range(groups)]
    zero = jnp.bfloat16(0)
    return [jnp.concatenate([jnp.where(m, f, zero) for m in masks], axis=0) for f in filled]


def split(cell):
    return ((cell >> 7) & 3) * 16 + (cell >> 9), cell & 127


def deposit_kernel(side_ref, counts_ref, cells_ref, dose_ref, out_ref):
    side = side_ref[0]
    slots = cells_ref.shape[1]

    def strip(j, carry):
        o = 2 * j + side
        count = counts_ref[o]
        total = jnp.zeros((2 * 64, LANES), F32)
        for k in range(0, slots, SPAN):
            cell = cells_ref[pl.ds(o, 1), k : k + SPAN]
            slot = lax.broadcasted_iota(jnp.int32, (1, SPAN), 1) + k
            dose = jnp.where(slot < count, dose_ref[pl.ds(o, 1), k : k + SPAN], 0.0)
            high = dose.astype(BF16).astype(F32)
            chunk, lane = split(cell)
            rows = hot(chunk, 4, [rows_of(high, BF16), rows_of(dose - high, BF16)])
            (cols,) = hot(lane, 8, [jnp.bfloat16(1)])
            total = total + lax.dot_general(
                jnp.concatenate(rows, axis=0),
                cols,
                (((1,), (1,)), ((), ())),
                preferred_element_type=F32,
            )
        both = total[:64] + total[64:]
        for q in range(4):
            out_ref[j, :, q * LANES : (q + 1) * LANES] = both[16 * q : 16 * q + 16]
        return carry

    lax.fori_loop(0, out_ref.shape[0], strip, 0)


def deposit(side, counts, cells, dose):
    return pl.pallas_call(
        deposit_kernel,
        out_shape=f32(8, 16, 512),
        in_specs=[SMEM, SMEM, VMEM, VMEM],
        out_specs=VMEM,
        compiler_params=PARAMS,
        cost_estimate=pl.CostEstimate(flops=1 << 30, bytes_accessed=1 << 19, transcendentals=0),
        name="deposit",
    )(side, counts, cells, dose)


def gather_kernel(coef_ref, parts_ref, materials_ref, target_ref, mid_ref, left_ref, right_ref):
    strip = parts_ref[0]
    for z in range(1, parts_ref.shape[0]):
        strip = strip + parts_ref[z]
    materials = materials_ref[...]
    spread = jnp.zeros(materials.shape, F32)
    for index in range(coef_ref.shape[0]):
        spread = jnp.where(materials == index, coef_ref[index], spread)
    for i, value in enumerate((strip, spread, target_ref[...])):
        mid_ref[i] = value
        left_ref[i] = value[:, :LANES]
        right_ref[i] = value[:, -LANES:]


def widen_kernel(mid_ref, left_ref, right_ref, wide_ref, top_ref, bottom_ref):
    for i in range(3):
        wide = jnp.concatenate([left_ref[i], mid_ref[i], right_ref[i]], axis=1)
        wide_ref[i] = wide
        if i == 0:
            top_ref[:8] = wide[:8]
            bottom_ref[:8] = wide[8:]
        elif i == 1:
            top_ref[8:13] = wide[:5]
            bottom_ref[11:] = wide[11:]
        else:
            top_ref[13:] = wide[:3]
            bottom_ref[8:11] = wide[13:]


def neighbours(field):
    height, width = field.shape
    return (
        pltpu.roll(field, 1, 0)
        + pltpu.roll(field, height - 1, 0)
        + pltpu.roll(field, 1, 1)
        + pltpu.roll(field, width - 1, 1)
    )


def blur_kernel(wide_ref, above_ref, below_ref, exposure_ref, adjoint_ref):
    width = wide_ref.shape[2]
    blank = lambda rows: jnp.zeros((rows, width), F32)
    field = jnp.concatenate([above_ref[:8], wide_ref[0], below_ref[:8]], axis=0)
    spread = jnp.concatenate(
        [blank(3), above_ref[11:], wide_ref[1], below_ref[8:13], blank(3)], axis=0
    )
    target = jnp.concatenate(
        [blank(5), above_ref[8:11], wide_ref[2], below_ref[13:], blank(5)], axis=0
    )
    for step in range(STEPS):
        field = field + spread * (neighbours(field) - 4.0 * field)
    exposure_ref[...] = field[8:24, LANES:-LANES]
    field = field - target
    for step in range(STEPS):
        weighted = spread * field
        field = field + neighbours(weighted) - 4.0 * weighted
    for q in range(4):
        adjoint_ref[16 * q : 16 * q + 16] = field[8:24, (q + 1) * LANES : (q + 2) * LANES]


def pick_kernel(counts_ref, cells_ref, table_ref, out_ref):
    slots = cells_ref.shape[1]

    def strip(o, carry):
        table = table_ref[pl.ds(pl.multiple_of(o * 64, 64), 64), :]
        high = table.astype(BF16)
        low = (table - high.astype(F32)).astype(BF16)
        both = jnp.concatenate([high, low], axis=0)
        count = counts_ref[o]
        for k in range(0, slots, SPAN):
            chunk, lane = split(cells_ref[pl.ds(o, 1), k : k + SPAN])
            (cols,) = hot(lane, 8, [jnp.bfloat16(1)])
            across = jnp.dot(both, cols, preferred_element_type=F32)
            across = across[:64] + across[64:]
            iota = lax.broadcasted_iota(jnp.int32, (8, SPAN), 0)
            chosen = jnp.broadcast_to(chunk, (8, SPAN))
            value = jnp.zeros((8, SPAN), F32)
            for g in range(8):
                value = jnp.where(chosen == iota + 8 * g, across[8 * g : 8 * g + 8], value)
            value = jnp.sum(value, axis=0, keepdims=True)
            slot = lax.broadcasted_iota(jnp.int32, (1, SPAN), 1) + k
            out_ref[pl.ds(o, 1), k : k + SPAN] = jnp.where(slot < count, value, 0.0)
        return carry

    lax.fori_loop(0, cells_ref.shape[0], strip, 0)


def pick(counts, cells, table):
    return pl.pallas_call(
        pick_kernel,
        out_shape=f32(*cells.shape),
        in_specs=[SMEM, VMEM, VMEM],
        out_specs=VMEM,
        compiler_params=PARAMS,
        name="pick",
    )(counts, cells, table)


def shifted(value, axes, count, by):
    return lax.ppermute(
        value, axes, [(i, i + by) for i in range(count) if 0 <= i + by < count]
    )


def local(shot_cells, shot_dose, shot_counts, materials, coefficients, target):
    cells, dose, counts = shot_cells[0, 0, 0], shot_dose[0, 0, 0], shot_counts[0, 0, 0]
    shots = lax.axis_size("shots")
    core = lax.axis_index("shots") % 2
    side = jnp.reshape(core, (1,)).astype(jnp.int32)
    away = deposit(1 - side, counts, cells, dose)
    arrived = lax.ppermute(away, "shots", [(i, i ^ 1) for i in range(shots)])
    own = deposit(side, counts, cells, dose)
    paired = own + arrived
    groups = [[2 * z + c for z in range(shots // 2)] for c in range(2)]
    parts = lax.all_to_all(paired, "shots", 0, 0, axis_index_groups=groups, tiled=True)
    mid, left, right = pl.pallas_call(
        gather_kernel,
        out_shape=(f32(3, 16, 512), f32(3, 16, LANES), f32(3, 16, LANES)),
        in_specs=[SMEM, VMEM, VMEM, VMEM],
        out_specs=(VMEM,) * 3,
        compiler_params=PARAMS,
        name="gather",
    )(coefficients, parts, materials, target)
    columns = lax.axis_size("gx")
    from_left = shifted(right, "gx", columns, 1)
    from_right = shifted(left, "gx", columns, -1)
    wide, top, bottom = pl.pallas_call(
        widen_kernel,
        out_shape=(f32(3, 16, 768), f32(16, 768), f32(16, 768)),
        in_specs=[VMEM] * 3,
        out_specs=(VMEM,) * 3,
        compiler_params=PARAMS,
        name="widen",
    )(mid, from_left, from_right)
    strips = shots * lax.axis_size("gy")
    above = shifted(bottom, ("shots", "gy"), strips, 1)
    below = shifted(top, ("shots", "gy"), strips, -1)
    exposure, adjoint = pl.pallas_call(
        blur_kernel,
        out_shape=(f32(16, 512), f32(64, LANES)),
        in_specs=[VMEM] * 3,
        out_specs=(VMEM,) * 2,
        compiler_params=PARAMS,
        name="blur",
    )(wide, above, below)
    table = lax.all_gather(adjoint, "shots", axis=0, tiled=True)
    shot_grad = pick(counts, cells, table)
    return (exposure, shot_grad[None, None, None])


def solution(mesh):
    placed = (
        P("shots", "gy", "gx", None, None),
        P("shots", "gy", "gx", None, None),
        P("shots", "gy", "gx", None),
        P(("shots", "gy"), "gx"),
        P(),
        P(("shots", "gy"), "gx"),
    )
    return jax.shard_map(
        local,
        mesh=mesh,
        in_specs=placed,
        out_specs=(P(("shots", "gy"), "gx"), P("shots", "gy", "gx", None, None)),
        check_vma=False,
    )
```

```python
import functools

import jax
import jax.numpy as jnp
from jax import lax
from jax.experimental import pallas as pl
from jax.experimental.pallas import tpu as pltpu
from jax.sharding import PartitionSpec as P

STEPS = 3
SPAN = 512
LANES = 128
VMEM = pl.BlockSpec(memory_space=pltpu.VMEM)
SMEM = pl.BlockSpec(memory_space=pltpu.SMEM)
PARAMS = pltpu.CompilerParams(vmem_limit_bytes=32 << 20)
F32 = jnp.float32
BF16 = jnp.bfloat16


def f32(*shape):
    return jax.ShapeDtypeStruct(shape, F32)


def rows_of(value, kind):
    return jnp.broadcast_to(value, (16, value.shape[1])).astype(kind)


def hot(index, groups, filled):
    width = index.shape[1]
    ids = rows_of(index, jnp.int16)
    iota = lax.broadcasted_iota(jnp.int16, (16, width), 0)
    masks = [ids == iota + jnp.int16(16 * g) for g in range(groups)]
    zero = jnp.bfloat16(0)
    return [jnp.concatenate([jnp.where(m, f, zero) for m in masks], axis=0) for f in filled]


COST = pl.CostEstimate(flops=1 << 30, bytes_accessed=1 << 18, transcendentals=0)


def split(cell):
    return ((cell >> 7) & 3) * 16 + (cell >> 9), cell & 127


def deposit_kernel(side, info_ref, counts_ref, cells_ref, dose_ref, out_ref):
    core = info_ref[0] ^ side
    slots = cells_ref.shape[1]

    def strip(j, carry):
        o = 2 * j + core
        count = counts_ref[o]
        total = jnp.zeros((2 * 64, LANES), F32)
        for k in range(0, slots, SPAN):
            cell = cells_ref[pl.ds(o, 1), k : k + SPAN]
            slot = lax.broadcasted_iota(jnp.int32, (1, SPAN), 1) + k
            dose = jnp.where(slot < count, dose_ref[pl.ds(o, 1), k : k + SPAN], 0.0)
            high = dose.astype(BF16).astype(F32)
            chunk, lane = split(cell)
            rows = hot(chunk, 4, [rows_of(high, BF16), rows_of(dose - high, BF16)])
            (cols,) = hot(lane, 8, [jnp.bfloat16(1)])
            total = total + lax.dot_general(
                jnp.concatenate(rows, axis=0),
                cols,
                (((1,), (1,)), ((), ())),
                preferred_element_type=F32,
            )
        both = total[:64] + total[64:]
        for q in range(4):
            out_ref[j, :, q * LANES : (q + 1) * LANES] = both[16 * q : 16 * q + 16]
        return carry

    lax.fori_loop(0, out_ref.shape[0], strip, 0, unroll=4)


def deposit(side, info, counts, cells, dose):
    return pl.pallas_call(
        functools.partial(deposit_kernel, side),
        out_shape=f32(8, 16, 512),
        in_specs=[SMEM, SMEM, VMEM, VMEM],
        out_specs=VMEM,
        compiler_params=PARAMS,
        cost_estimate=pl.CostEstimate(flops=1 << 30, bytes_accessed=1 << 19, transcendentals=0),
        name="deposit",
    )(info, counts, cells, dose)


def gather_kernel(info_ref, coef_ref, parts_ref, materials_ref, target_ref, *outs):
    mid_ref, first_ref, second_ref = outs
    even = info_ref[1] == 0
    strip = parts_ref[0]
    for z in range(1, parts_ref.shape[0]):
        strip = strip + parts_ref[z]
    materials = materials_ref[...]
    spread = jnp.zeros(materials.shape, F32)
    for index in range(coef_ref.shape[0]):
        spread = jnp.where(materials == index, coef_ref[index], spread)
    for i, value in enumerate((strip, spread, target_ref[...])):
        mid_ref[i] = value
        left, right = value[:, :LANES], value[:, -LANES:]
        first_ref[i] = jnp.where(even, right, left)
        second_ref[i] = jnp.where(even, left, right)


def widen_kernel(info_ref, mid_ref, first_ref, second_ref, wide_ref, send_ref, later_ref):
    even, even_y = info_ref[1] == 0, info_ref[2] == 0
    near = lax.broadcasted_iota(jnp.int32, (16, LANES), 1) < LANES // 2
    for i in range(3):
        first, second = first_ref[i], second_ref[i]
        left = jnp.where(even, second, first)
        right = jnp.where(even, first, second)
        wide = jnp.concatenate([mid_ref[i], jnp.where(near, right, left)], axis=1)
        wide_ref[i] = wide
        if i == 0:
            top, bottom = wide[:8], wide[8:]
        elif i == 1:
            top, bottom = jnp.concatenate([top, wide[:5]]), jnp.concatenate([bottom, wide[11:]])
        else:
            top, bottom = jnp.concatenate([top, wide[:3]]), jnp.concatenate([bottom, wide[13:]])
    send_ref[...] = jnp.where(even_y, bottom, top)
    later_ref[...] = jnp.where(even_y, top, bottom)


def neighbours(field):
    height, width = field.shape
    return (
        pltpu.roll(field, 1, 0)
        + pltpu.roll(field, height - 1, 0)
        + pltpu.roll(field, 1, 1)
        + pltpu.roll(field, width - 1, 1)
    )


def blur_kernel(info_ref, wide_ref, first_ref, second_ref, exposure_ref, adjoint_ref):
    even = info_ref[2] == 0
    first, second = first_ref[...], second_ref[...]
    above, below = jnp.where(even, second, first), jnp.where(even, first, second)
    width = wide_ref.shape[2]
    blank = lambda rows: jnp.zeros((rows, width), F32)
    field = jnp.concatenate([above[:8], wide_ref[0], below[:8]], axis=0)
    spread = jnp.concatenate(
        [blank(3), above[8:13], wide_ref[1], below[8:13], blank(3)], axis=0
    )
    target = jnp.concatenate(
        [blank(5), above[13:], wide_ref[2], below[13:], blank(5)], axis=0
    )
    for step in range(STEPS):
        field = field + spread * (neighbours(field) - 4.0 * field)
    exposure_ref[...] = field[8:24, :-LANES]
    field = field - target
    for step in range(STEPS):
        weighted = spread * field
        field = field + neighbours(weighted) - 4.0 * weighted
    for q in range(4):
        for z in range(adjoint_ref.shape[0]):
            adjoint_ref[z, 16 * q : 16 * q + 16] = field[8:24, q * LANES : (q + 1) * LANES]


def pick_strips(core, counts_ref, cells_ref, table_ref, store):
    slots = cells_ref.shape[1]

    def strip(z, carry):
        o = 2 * z + core
        table = table_ref[z]
        high = table.astype(BF16)
        low = (table - high.astype(F32)).astype(BF16)
        both = jnp.concatenate([high, low], axis=0)
        count = counts_ref[o]
        for k in range(0, slots, SPAN):
            chunk, lane = split(cells_ref[pl.ds(o, 1), k : k + SPAN])
            (cols,) = hot(lane, 8, [jnp.bfloat16(1)])
            across = jnp.dot(both, cols, preferred_element_type=F32)
            across = across[:64] + across[64:]
            iota = lax.broadcasted_iota(jnp.int32, (8, SPAN), 0)
            chosen = jnp.broadcast_to(chunk, (8, SPAN))
            value = jnp.zeros((8, SPAN), F32)
            for g in range(8):
                value = jnp.where(chosen == iota + 8 * g, across[8 * g : 8 * g + 8], value)
            value = jnp.sum(value, axis=0, keepdims=True)
            slot = lax.broadcasted_iota(jnp.int32, (1, SPAN), 1) + k
            store(z, o, k, jnp.where(slot < count, value, 0.0))
        return carry

    lax.fori_loop(0, table_ref.shape[0], strip, 0, unroll=4)


def pick_kernel(info_ref, counts_ref, cells_ref, table_ref, out_ref):
    def store(z, o, k, value):
        out_ref[pl.ds(z, 1), k : k + SPAN] = value

    pick_strips(info_ref[0], counts_ref, cells_ref, table_ref, store)


def last_kernel(info_ref, counts_ref, cells_ref, table_ref, own_ref, out_ref):
    def store(z, o, k, value):
        out_ref[pl.ds(o, 1), k : k + SPAN] = value

    pick_strips(1 - info_ref[0], counts_ref, cells_ref, table_ref, store)
    for z in range(own_ref.shape[0]):
        out_ref[pl.ds(2 * z + info_ref[0], 1), :] = own_ref[z : z + 1, :]


def pick(info, counts, cells, table, own=None):
    last = own is not None
    return pl.pallas_call(
        last_kernel if last else pick_kernel,
        out_shape=f32(cells.shape[0] if last else table.shape[0], cells.shape[1]),
        in_specs=[SMEM, SMEM] + [VMEM] * (3 if last else 2),
        out_specs=VMEM,
        compiler_params=PARAMS,
        cost_estimate=COST,
        name="pick_last" if last else "pick",
    )(info, counts, cells, table, *([own] if last else []))


def swap(value, axes, bits):
    count = lax.axis_size(axes)
    return lax.ppermute(value, axes, [(i, i ^ bits) for i in range(count)])


def swap_later(value, axes):
    count = lax.axis_size(axes)
    pairs = [(i, i + 1) for i in range(1, count - 1, 2)]
    return lax.ppermute(value, axes, pairs + [(j, i) for i, j in pairs])


def local(shot_cells, shot_dose, shot_counts, materials, coefficients, target):
    cells, dose, counts = shot_cells[0, 0, 0], shot_dose[0, 0, 0], shot_counts[0, 0, 0]
    shots = lax.axis_size("shots")
    info = jnp.stack(
        [lax.axis_index("shots") % 2, lax.axis_index("gx") % 2, lax.axis_index("gy") % 2]
    ).astype(jnp.int32)
    lines = [[2 * z + c for z in range(shots // 2)] for c in range(2)]

    def exchange(value):
        return lax.all_to_all(value, "shots", 0, 0, axis_index_groups=lines, tiled=True)

    away = swap(deposit(1, info, counts, cells, dose), "shots", 1)
    parts = exchange(deposit(0, info, counts, cells, dose) + away)

    mid, first, second = pl.pallas_call(
        gather_kernel,
        out_shape=(f32(3, 16, 512), f32(3, 16, LANES), f32(3, 16, LANES)),
        in_specs=[SMEM] * 2 + [VMEM] * 3,
        out_specs=(VMEM,) * 3,
        compiler_params=PARAMS,
        name="gather",
    )(info, coefficients, parts, materials, target)
    wide, first, second = pl.pallas_call(
        widen_kernel,
        out_shape=(f32(3, 16, 640), f32(16, 640), f32(16, 640)),
        in_specs=[SMEM] + [VMEM] * 3,
        out_specs=(VMEM,) * 3,
        compiler_params=PARAMS,
        name="widen",
    )(info, mid, swap(first, "gx", 1), swap_later(second, "gx"))
    rows = ("shots", "gy")
    exposure, adjoint = pl.pallas_call(
        blur_kernel,
        out_shape=(f32(16, 512), f32(shots // 2, 64, LANES)),
        in_specs=[SMEM] + [VMEM] * 3,
        out_specs=(VMEM,) * 2,
        compiler_params=PARAMS,
        name="blur",
    )(info, wide, swap(first, rows, 1), swap_later(second, rows))

    table = exchange(adjoint)
    other = swap(table, "shots", 1)
    shot_grad = pick(info, counts, cells, other, pick(info, counts, cells, table))
    return (exposure, shot_grad[None, None, None])


def solution(mesh):
    placed = (
        P("shots", "gy", "gx", None, None),
        P("shots", "gy", "gx", None, None),
        P("shots", "gy", "gx", None),
        P(("shots", "gy"), "gx"),
        P(),
        P(("shots", "gy"), "gx"),
    )
    return jax.shard_map(
        local,
        mesh=mesh,
        in_specs=placed,
        out_specs=(P(("shots", "gy"), "gx"), P("shots", "gy", "gx", None, None)),
        check_vma=False,
    )
```

```python
import functools

import jax
import jax.numpy as jnp
from jax import lax
from jax.experimental import pallas as pl
from jax.experimental.pallas import tpu as pltpu
from jax.sharding import PartitionSpec as P

STEPS = 3
SPAN = 512
LANES = 128
VMEM = pl.BlockSpec(memory_space=pltpu.VMEM)
HBM = pl.BlockSpec(memory_space=pltpu.HBM)
PARAMS = pltpu.CompilerParams(vmem_limit_bytes=32 << 20)
F32 = jnp.float32
BF16 = jnp.bfloat16


def f32(*shape):
    return jax.ShapeDtypeStruct(shape, F32)


def rows_of(value, kind):
    return jnp.broadcast_to(value, (16, value.shape[1])).astype(kind)


def hot(index, groups, filled):
    width = index.shape[1]
    ids = rows_of(index, jnp.int16)
    iota = lax.broadcasted_iota(jnp.int16, (16, width), 0)
    masks = [ids == iota + jnp.int16(16 * g) for g in range(groups)]
    zero = jnp.bfloat16(0)
    return [jnp.concatenate([jnp.where(m, f, zero) for m in masks], axis=0) for f in filled]


COST = pl.CostEstimate(flops=1 << 30, bytes_accessed=1 << 18, transcendentals=0)


def split(cell):
    return ((cell >> 7) & 3) * 16 + (cell >> 9), cell & 127


def own_core():
    return lax.axis_index("shots") % 2


def alive(counts_ref, strip, k):
    count = jnp.concatenate([counts_ref[pl.ds(strip, 1), :]] * (SPAN // LANES), axis=1)
    return lax.broadcasted_iota(jnp.int32, (1, SPAN), 1) + k < count


def deposit_kernel(side, counts_ref, cells_ref, dose_ref, out_ref):
    core = own_core() ^ side
    slots = cells_ref.shape[1]

    def strip(j, carry):
        o = 2 * j + core
        total = jnp.zeros((2 * 64, LANES), F32)
        for k in range(0, slots, SPAN):
            cell = cells_ref[pl.ds(o, 1), k : k + SPAN]
            dose = jnp.where(alive(counts_ref, o, k), dose_ref[pl.ds(o, 1), k : k + SPAN], 0.0)
            high = dose.astype(BF16).astype(F32)
            chunk, lane = split(cell)
            rows = hot(chunk, 4, [rows_of(high, BF16), rows_of(dose - high, BF16)])
            (cols,) = hot(lane, 8, [jnp.bfloat16(1)])
            total = total + lax.dot_general(
                jnp.concatenate(rows, axis=0),
                cols,
                (((1,), (1,)), ((), ())),
                preferred_element_type=F32,
            )
        both = total[:64] + total[64:]
        for q in range(4):
            out_ref[j, :, q * LANES : (q + 1) * LANES] = both[16 * q : 16 * q + 16]
        return carry

    lax.fori_loop(0, out_ref.shape[0], strip, 0, unroll=4)


def first_kernel(*refs):
    sources, (out_ref, counts_ref, cells, dose, spread_ref) = refs[:5], refs[5:10]
    counts, materials, coefs, sems = refs[10:]
    targets = (counts, coefs, cells, dose, materials)
    copies = [
        pltpu.make_async_copy(source, target, sems.at[i])
        for i, (source, target) in enumerate(zip(sources, targets))
    ]
    for copy in copies:
        copy.start()
    for copy in copies:
        copy.wait()
    for o in range(counts_ref.shape[0]):
        counts_ref[o : o + 1, :] = jnp.full((1, LANES), counts[o], jnp.int32)
    spread = jnp.zeros(materials.shape, F32)
    for index in range(coefs.shape[0]):
        spread = jnp.where(materials[...] == index, coefs[index], spread)
    spread_ref[...] = spread
    deposit_kernel(1, counts_ref, cells, dose, out_ref)


def deposit_first(counts, coefficients, cells, dose, materials):
    inputs = (counts, coefficients, cells, dose, materials)
    same = lambda value: jax.ShapeDtypeStruct(value.shape, value.dtype)
    return pl.pallas_call(
        first_kernel,
        out_shape=(
            f32(8, 16, 512),
            jax.ShapeDtypeStruct((counts.shape[0], LANES), jnp.int32),
            same(cells),
            same(dose),
            f32(*materials.shape),
        ),
        in_specs=[HBM] * 5,
        out_specs=(VMEM,) * 5,
        scratch_shapes=[
            pltpu.SMEM(counts.shape, jnp.int32),
            pltpu.VMEM(materials.shape, jnp.int32),
            pltpu.SMEM(coefficients.shape, F32),
            pltpu.SemaphoreType.DMA((5,)),
        ],
        compiler_params=PARAMS,
        cost_estimate=COST,
        name="deposit_first",
    )(*(pltpu.with_memory_space_constraint(value, pltpu.HBM) for value in inputs))


def deposit(counts, cells, dose):
    return pl.pallas_call(
        functools.partial(deposit_kernel, 0),
        out_shape=f32(8, 16, 512),
        in_specs=[VMEM] * 3,
        out_specs=VMEM,
        compiler_params=PARAMS,
        cost_estimate=COST,
        name="deposit",
    )(counts, cells, dose)


def gather_kernel(parts_ref, spread_ref, target_ref, mid_ref, first_ref, second_ref):
    even = lax.axis_index("gx") % 2 == 0
    strip = parts_ref[0]
    for z in range(1, parts_ref.shape[0]):
        strip = strip + parts_ref[z]
    for i, value in enumerate((strip, spread_ref[...], target_ref[...])):
        mid_ref[i] = value
        left, right = value[:, :LANES], value[:, -LANES:]
        first_ref[i] = jnp.where(even, right, left)
        second_ref[i] = jnp.where(even, left, right)


def widen_kernel(mid_ref, first_ref, second_ref, wide_ref, send_ref, later_ref):
    even, even_y = lax.axis_index("gx") % 2 == 0, lax.axis_index("gy") % 2 == 0
    near = lax.broadcasted_iota(jnp.int32, (16, LANES), 1) < LANES // 2
    for i in range(3):
        first, second = first_ref[i], second_ref[i]
        left = jnp.where(even, second, first)
        right = jnp.where(even, first, second)
        wide = jnp.concatenate([mid_ref[i], jnp.where(near, right, left)], axis=1)
        wide_ref[i] = wide
        if i == 0:
            top, bottom = wide[:8], wide[8:]
        elif i == 1:
            top, bottom = jnp.concatenate([top, wide[:5]]), jnp.concatenate([bottom, wide[11:]])
        else:
            top, bottom = jnp.concatenate([top, wide[:3]]), jnp.concatenate([bottom, wide[13:]])
    send_ref[...] = jnp.where(even_y, bottom, top)
    later_ref[...] = jnp.where(even_y, top, bottom)


def neighbours(field):
    height, width = field.shape
    return (
        pltpu.roll(field, 1, 0)
        + pltpu.roll(field, height - 1, 0)
        + pltpu.roll(field, 1, 1)
        + pltpu.roll(field, width - 1, 1)
    )


def blur_kernel(wide_ref, first_ref, second_ref, exposure_ref, adjoint_ref):
    even = lax.axis_index("gy") % 2 == 0
    first, second = first_ref[...], second_ref[...]
    above, below = jnp.where(even, second, first), jnp.where(even, first, second)
    width = wide_ref.shape[2]
    blank = lambda rows: jnp.zeros((rows, width), F32)
    field = jnp.concatenate([above[:8], wide_ref[0], below[:8]], axis=0)
    spread = jnp.concatenate(
        [blank(3), above[8:13], wide_ref[1], below[8:13], blank(3)], axis=0
    )
    target = jnp.concatenate(
        [blank(5), above[13:], wide_ref[2], below[13:], blank(5)], axis=0
    )
    for step in range(STEPS):
        field = field + spread * (neighbours(field) - 4.0 * field)
    exposure_ref[...] = field[8:24, :-LANES]
    field = field - target
    for step in range(STEPS):
        weighted = spread * field
        field = field + neighbours(weighted) - 4.0 * weighted
    for q in range(4):
        for z in range(adjoint_ref.shape[0]):
            adjoint_ref[z, 16 * q : 16 * q + 16] = field[8:24, q * LANES : (q + 1) * LANES]


def pick_strips(core, counts_ref, cells_ref, table_ref, store):
    slots = cells_ref.shape[1]

    def strip(z, carry):
        o = 2 * z + core
        table = table_ref[z]
        high = table.astype(BF16)
        low = (table - high.astype(F32)).astype(BF16)
        both = jnp.concatenate([high, low], axis=0)
        for k in range(0, slots, SPAN):
            chunk, lane = split(cells_ref[pl.ds(o, 1), k : k + SPAN])
            (cols,) = hot(lane, 8, [jnp.bfloat16(1)])
            across = jnp.dot(both, cols, preferred_element_type=F32)
            across = across[:64] + across[64:]
            iota = lax.broadcasted_iota(jnp.int32, (8, SPAN), 0)
            chosen = jnp.broadcast_to(chunk, (8, SPAN))
            value = jnp.zeros((8, SPAN), F32)
            for g in range(8):
                value = jnp.where(chosen == iota + 8 * g, across[8 * g : 8 * g + 8], value)
            value = jnp.sum(value, axis=0, keepdims=True)
            store(z, o, k, jnp.where(alive(counts_ref, o, k), value, 0.0))
        return carry

    lax.fori_loop(0, table_ref.shape[0], strip, 0, unroll=4)


def pick_kernel(counts_ref, cells_ref, table_ref, out_ref):
    def store(z, o, k, value):
        out_ref[pl.ds(z, 1), k : k + SPAN] = value

    pick_strips(own_core(), counts_ref, cells_ref, table_ref, store)


def last_kernel(counts_ref, cells_ref, table_ref, own_ref, out_ref):
    def store(z, o, k, value):
        out_ref[pl.ds(o, 1), k : k + SPAN] = value

    pick_strips(1 - own_core(), counts_ref, cells_ref, table_ref, store)
    for z in range(own_ref.shape[0]):
        out_ref[pl.ds(2 * z + own_core(), 1), :] = own_ref[z : z + 1, :]


def pick(counts, cells, table, own=None):
    last = own is not None
    return pl.pallas_call(
        last_kernel if last else pick_kernel,
        out_shape=f32(cells.shape[0] if last else table.shape[0], cells.shape[1]),
        in_specs=[VMEM] * (4 if last else 3),
        out_specs=VMEM,
        compiler_params=PARAMS,
        cost_estimate=COST,
        name="pick_last" if last else "pick",
    )(counts, cells, table, *([own] if last else []))


def swap(value, axes, bits):
    count = lax.axis_size(axes)
    return lax.ppermute(value, axes, [(i, i ^ bits) for i in range(count)])


def swap_later(value, axes):
    count = lax.axis_size(axes)
    pairs = [(i, i + 1) for i in range(1, count - 1, 2)]
    return lax.ppermute(value, axes, pairs + [(j, i) for i, j in pairs])


def local(shot_cells, shot_dose, shot_counts, materials, coefficients, target):
    cells, dose, counts = shot_cells[0, 0, 0], shot_dose[0, 0, 0], shot_counts[0, 0, 0]
    shots = lax.axis_size("shots")
    lines = [[2 * z + c for z in range(shots // 2)] for c in range(2)]

    def exchange(value):
        return lax.all_to_all(value, "shots", 0, 0, axis_index_groups=lines, tiled=True)

    away, counts, cells, dose, spread = deposit_first(
        counts, coefficients, cells, dose, materials
    )
    away = swap(away, "shots", 1)
    parts = exchange(deposit(counts, cells, dose) + away)

    mid, first, second = pl.pallas_call(
        gather_kernel,
        out_shape=(f32(3, 16, 512), f32(3, 16, LANES), f32(3, 16, LANES)),
        in_specs=[VMEM] * 3,
        out_specs=(VMEM,) * 3,
        compiler_params=PARAMS,
        name="gather",
    )(parts, spread, target)
    wide, first, second = pl.pallas_call(
        widen_kernel,
        out_shape=(f32(3, 16, 640), f32(16, 640), f32(16, 640)),
        in_specs=[VMEM] * 3,
        out_specs=(VMEM,) * 3,
        compiler_params=PARAMS,
        name="widen",
    )(mid, swap(first, "gx", 1), swap_later(second, "gx"))
    rows = ("shots", "gy")
    exposure, adjoint = pl.pallas_call(
        blur_kernel,
        out_shape=(f32(16, 512), f32(shots // 2, 64, LANES)),
        in_specs=[VMEM] * 3,
        out_specs=(VMEM,) * 2,
        compiler_params=PARAMS,
        name="blur",
    )(wide, swap(first, rows, 1), swap_later(second, rows))

    table = exchange(adjoint)
    other = swap(table, "shots", 1)
    shot_grad = pick(counts, cells, other, pick(counts, cells, table))
    return (exposure, shot_grad[None, None, None])


def solution(mesh):
    placed = (
        P("shots", "gy", "gx", None, None),
        P("shots", "gy", "gx", None, None),
        P("shots", "gy", "gx", None),
        P(("shots", "gy"), "gx"),
        P(),
        P(("shots", "gy"), "gx"),
    )
    return jax.shard_map(
        local,
        mesh=mesh,
        in_specs=placed,
        out_specs=(P(("shots", "gy"), "gx"), P("shots", "gy", "gx", None, None)),
        check_vma=False,
    )
```

```python
import functools

import jax
import jax.numpy as jnp
from jax import lax
from jax.experimental import pallas as pl
from jax.experimental.pallas import tpu as pltpu
from jax.sharding import PartitionSpec as P

STEPS = 3
SPAN = 512
CHUNK = 1024
UNROLL = 8
LANES = 128
VMEM = pl.BlockSpec(memory_space=pltpu.VMEM)
HBM = pl.BlockSpec(memory_space=pltpu.HBM)
PARAMS = pltpu.CompilerParams(vmem_limit_bytes=32 << 20)
F32 = jnp.float32
BF16 = jnp.bfloat16


def f32(*shape):
    return jax.ShapeDtypeStruct(shape, F32)


def rows_of(value, kind):
    return jnp.broadcast_to(value, (16, value.shape[1])).astype(kind)


def hot(index, groups, filled):
    width = index.shape[1]
    ids = rows_of(index, jnp.int16)
    iota = lax.broadcasted_iota(jnp.int16, (16, width), 0)
    masks = [ids == iota + jnp.int16(16 * g) for g in range(groups)]
    zero = jnp.bfloat16(0)
    return [jnp.concatenate([jnp.where(m, f, zero) for m in masks], axis=0) for f in filled]


COST = pl.CostEstimate(flops=1 << 30, bytes_accessed=1 << 18, transcendentals=0)


def split(cell):
    return ((cell >> 7) & 3) * 16 + (cell >> 9), cell & 127


def own_core():
    return lax.axis_index("shots") % 2


def alive(counts_ref, strip, k):
    count = jnp.concatenate([counts_ref[pl.ds(strip, 1), :]] * (SPAN // LANES), axis=1)
    return lax.broadcasted_iota(jnp.int32, (1, SPAN), 1) + k < count


def deposit_kernel(side, counts_ref, cells_ref, dose_ref, out_ref):
    core = own_core() ^ side
    slots = cells_ref.shape[1]

    def strip(j, carry):
        o = 2 * j + core
        total = jnp.zeros((2 * 64, LANES), F32)
        for k in range(0, slots, SPAN):
            cell = cells_ref[pl.ds(o, 1), k : k + SPAN]
            dose = jnp.where(alive(counts_ref, o, k), dose_ref[pl.ds(o, 1), k : k + SPAN], 0.0)
            high = dose.astype(BF16).astype(F32)
            chunk, lane = split(cell)
            rows = hot(chunk, 4, [rows_of(high, BF16), rows_of(dose - high, BF16)])
            (cols,) = hot(lane, 8, [jnp.bfloat16(1)])
            total = total + lax.dot_general(
                jnp.concatenate(rows, axis=0),
                cols,
                (((1,), (1,)), ((), ())),
                preferred_element_type=F32,
            )
        both = total[:64] + total[64:]
        for q in range(4):
            out_ref[j, :, q * LANES : (q + 1) * LANES] = both[16 * q : 16 * q + 16]
        return carry

    lax.fori_loop(0, out_ref.shape[0], strip, 0, unroll=UNROLL)


def first_kernel(*refs):
    sources, (out_ref, counts_ref, cells, dose, spread_ref) = refs[:5], refs[5:10]
    counts, materials, coefs, sems = refs[10:]
    targets = (counts, coefs, cells, dose, materials)
    copies = [
        pltpu.make_async_copy(source, target, sems.at[i])
        for i, (source, target) in enumerate(zip(sources, targets))
    ]
    for copy in copies:
        copy.start()
    for copy in copies:
        copy.wait()
    for o in range(counts_ref.shape[0]):
        counts_ref[o : o + 1, :] = jnp.full((1, LANES), counts[o], jnp.int32)
    spread = jnp.zeros(materials.shape, F32)
    for index in range(coefs.shape[0]):
        spread = jnp.where(materials[...] == index, coefs[index], spread)
    spread_ref[...] = spread
    deposit_kernel(1, counts_ref, cells, dose, out_ref)


def deposit_first(counts, coefficients, cells, dose, materials):
    inputs = (counts, coefficients, cells, dose, materials)
    same = lambda value: jax.ShapeDtypeStruct(value.shape, value.dtype)
    return pl.pallas_call(
        first_kernel,
        out_shape=(
            f32(8, 16, 512),
            jax.ShapeDtypeStruct((counts.shape[0], LANES), jnp.int32),
            same(cells),
            same(dose),
            f32(*materials.shape),
        ),
        in_specs=[HBM] * 5,
        out_specs=(VMEM,) * 5,
        scratch_shapes=[
            pltpu.SMEM(counts.shape, jnp.int32),
            pltpu.VMEM(materials.shape, jnp.int32),
            pltpu.SMEM(coefficients.shape, F32),
            pltpu.SemaphoreType.DMA((5,)),
        ],
        compiler_params=PARAMS,
        cost_estimate=COST,
        name="deposit_first",
    )(*(pltpu.with_memory_space_constraint(value, pltpu.HBM) for value in inputs))


def deposit(counts, cells, dose):
    return pl.pallas_call(
        functools.partial(deposit_kernel, 0),
        out_shape=f32(8, 16, 512),
        in_specs=[VMEM] * 3,
        out_specs=VMEM,
        compiler_params=PARAMS,
        cost_estimate=COST,
        name="deposit",
    )(counts, cells, dose)


def gather_kernel(parts_ref, spread_ref, target_ref, mid_ref, first_ref, second_ref):
    even = lax.axis_index("gx") % 2 == 0
    strip = parts_ref[0]
    for z in range(1, parts_ref.shape[0]):
        strip = strip + parts_ref[z]
    lane = lax.broadcasted_iota(jnp.int32, (16, LANES), 1)
    left, right = jnp.zeros((16, LANES), F32), jnp.zeros((16, LANES), F32)
    for i, value in enumerate((strip, spread_ref[...], target_ref[...])):
        mid_ref[i] = value
        here = (lane >= 16 * i) & (lane < 16 * i + 8)
        left = jnp.where(here, pltpu.roll(value[:, :LANES], 16 * i, 1), left)
        right = jnp.where(here, pltpu.roll(value[:, -LANES:], 16 * i + 8, 1), right)
    first_ref[...] = jnp.where(even, right, left)
    second_ref[...] = jnp.where(even, left, right)


def widen_kernel(mid_ref, first_ref, second_ref, wide_ref, send_ref, later_ref):
    even, even_y = lax.axis_index("gx") % 2 == 0, lax.axis_index("gy") % 2 == 0
    near = lax.broadcasted_iota(jnp.int32, (16, LANES), 1) < LANES // 2
    first, second = first_ref[...], second_ref[...]
    left, right = jnp.where(even, second, first), jnp.where(even, first, second)
    for i in range(3):
        tile = jnp.where(
            near,
            pltpu.roll(right, (LANES - 16 * i) % LANES, 1),
            pltpu.roll(left, LANES - 8 - 16 * i, 1),
        )
        wide = jnp.concatenate([mid_ref[i], tile], axis=1)
        wide_ref[i] = wide
        if i == 0:
            top, bottom = wide[:8], wide[8:]
        elif i == 1:
            top, bottom = jnp.concatenate([top, wide[:5]]), jnp.concatenate([bottom, wide[11:]])
        else:
            top, bottom = jnp.concatenate([top, wide[:3]]), jnp.concatenate([bottom, wide[13:]])
    send_ref[...] = jnp.where(even_y, bottom, top)
    later_ref[...] = jnp.where(even_y, top, bottom)


def neighbours(field):
    height, width = field.shape
    return (
        pltpu.roll(field, 1, 0)
        + pltpu.roll(field, height - 1, 0)
        + pltpu.roll(field, 1, 1)
        + pltpu.roll(field, width - 1, 1)
    )


def blur_kernel(wide_ref, first_ref, second_ref, exposure_ref, adjoint_ref):
    even = lax.axis_index("gy") % 2 == 0
    first, second = first_ref[...], second_ref[...]
    above, below = jnp.where(even, second, first), jnp.where(even, first, second)
    width = wide_ref.shape[2]
    blank = lambda rows: jnp.zeros((rows, width), F32)
    field = jnp.concatenate([above[:8], wide_ref[0], below[:8]], axis=0)
    spread = jnp.concatenate(
        [blank(3), above[8:13], wide_ref[1], below[8:13], blank(3)], axis=0
    )
    target = jnp.concatenate(
        [blank(5), above[13:], wide_ref[2], below[13:], blank(5)], axis=0
    )
    for step in range(STEPS):
        field = field + spread * (neighbours(field) - 4.0 * field)
    exposure_ref[...] = field[8:24, :-LANES]
    field = field - target
    for step in range(STEPS):
        weighted = spread * field
        field = field + neighbours(weighted) - 4.0 * weighted
    for q in range(4):
        for z in range(adjoint_ref.shape[0]):
            adjoint_ref[z, 16 * q : 16 * q + 16] = field[8:24, q * LANES : (q + 1) * LANES]


def parts_of(table):
    high = table.astype(BF16)
    return jnp.concatenate([high, (table - high.astype(F32)).astype(BF16)], axis=0)


def pick_span(counts_ref, cells_ref, both, o, k):
    span = pl.ds(k, SPAN)
    chunk, lane = split(cells_ref[pl.ds(o, 1), span])
    (cols,) = hot(lane, 8, [jnp.bfloat16(1)])
    across = jnp.dot(both, cols, preferred_element_type=F32)
    across = across[:64] + across[64:]
    iota = lax.broadcasted_iota(jnp.int32, (8, SPAN), 0)
    chosen = jnp.broadcast_to(chunk, (8, SPAN))
    value = jnp.zeros((8, SPAN), F32)
    for g in range(8):
        value = jnp.where(chosen == iota + 8 * g, across[8 * g : 8 * g + 8], value)
    value = jnp.sum(value, axis=0, keepdims=True)
    return jnp.where(alive(counts_ref, o, k), value, 0.0)


def pick_kernel(counts_ref, cells_ref, table_ref, blurred_ref, own_ref, exposure_hbm, sem):
    copy = pltpu.make_async_copy(blurred_ref, exposure_hbm, sem)
    copy.start()

    def strip(z, carry):
        both = parts_of(table_ref[z])
        for k in range(0, cells_ref.shape[1], SPAN):
            value = pick_span(counts_ref, cells_ref, both, 2 * z + own_core(), k)
            own_ref[pl.ds(z, 1), k : k + SPAN] = value
        return carry

    lax.fori_loop(0, table_ref.shape[0], strip, 0, unroll=UNROLL)
    copy.wait()


def pick(counts, cells, table, blurred):
    return pl.pallas_call(
        pick_kernel,
        out_shape=(f32(table.shape[0], cells.shape[1]), f32(*blurred.shape)),
        in_specs=[VMEM] * 4,
        out_specs=(VMEM, pl.BlockSpec(memory_space=pl.ANY)),
        scratch_shapes=[pltpu.SemaphoreType.DMA],
        compiler_params=PARAMS,
        cost_estimate=COST,
        name="pick",
    )(counts, cells, table, blurred)


def last_kernel(counts_ref, cells_ref, table_ref, own_ref, out_hbm, out_ref, both_ref, sems):
    depth, core = table_ref.shape[0], own_core()
    for z in range(depth):
        out_ref[pl.ds(2 * z + core, 1), :] = own_ref[z : z + 1, :]
        both_ref[z] = parts_of(table_ref[z])

    def copy(i):
        part = pl.ds(pl.multiple_of(i * CHUNK, CHUNK), CHUNK)
        return pltpu.make_async_copy(out_ref.at[:, part], out_hbm.at[:, part], sems.at[i])

    def chunk(i, carry):
        for z in range(depth):
            o = 2 * z + 1 - core
            for j in range(0, CHUNK, SPAN):
                k = pl.multiple_of(i * CHUNK + j, SPAN)
                value = pick_span(counts_ref, cells_ref, both_ref[z], o, k)
                out_ref[pl.ds(o, 1), pl.ds(k, SPAN)] = value
        copy(i).start()
        return carry

    steps = cells_ref.shape[1] // CHUNK
    lax.fori_loop(0, steps, chunk, 0, unroll=True)
    for i in range(steps):
        copy(i).wait()


def pick_last(counts, cells, table, own):
    return pl.pallas_call(
        last_kernel,
        out_shape=f32(*cells.shape),
        in_specs=[VMEM] * 4,
        out_specs=pl.BlockSpec(memory_space=pl.ANY),
        scratch_shapes=[
            pltpu.VMEM(cells.shape, F32),
            pltpu.VMEM((table.shape[0], 2 * 64, LANES), BF16),
            pltpu.SemaphoreType.DMA((cells.shape[1] // CHUNK,)),
        ],
        compiler_params=PARAMS,
        cost_estimate=COST,
        name="pick_last",
    )(counts, cells, table, own)


def swap(value, axes, bits):
    count = lax.axis_size(axes)
    return lax.ppermute(value, axes, [(i, i ^ bits) for i in range(count)])


def swap_later(value, axes):
    count = lax.axis_size(axes)
    pairs = [(i, i + 1) for i in range(1, count - 1, 2)]
    return lax.ppermute(value, axes, pairs + [(j, i) for i, j in pairs])


def local(shot_cells, shot_dose, shot_counts, materials, coefficients, target):
    cells, dose, counts = shot_cells[0, 0, 0], shot_dose[0, 0, 0], shot_counts[0, 0, 0]
    shots = lax.axis_size("shots")
    lines = [[2 * z + c for z in range(shots // 2)] for c in range(2)]

    def exchange(value):
        return lax.all_to_all(value, "shots", 0, 0, axis_index_groups=lines, tiled=True)

    away, counts, cells, dose, spread = deposit_first(
        counts, coefficients, cells, dose, materials
    )
    away = swap(away, "shots", 1)
    parts = exchange(deposit(counts, cells, dose) + away)

    mid, first, second = pl.pallas_call(
        gather_kernel,
        out_shape=(f32(3, 16, 512), f32(16, LANES), f32(16, LANES)),
        in_specs=[VMEM] * 3,
        out_specs=(VMEM,) * 3,
        compiler_params=PARAMS,
        name="gather",
    )(parts, spread, target)
    wide, first, second = pl.pallas_call(
        widen_kernel,
        out_shape=(f32(3, 16, 640), f32(16, 640), f32(16, 640)),
        in_specs=[VMEM] * 3,
        out_specs=(VMEM,) * 3,
        compiler_params=PARAMS,
        name="widen",
    )(mid, swap(first, "gx", 1), swap_later(second, "gx"))
    rows = ("shots", "gy")
    blurred, adjoint = pl.pallas_call(
        blur_kernel,
        out_shape=(f32(16, 512), f32(shots // 2, 64, LANES)),
        in_specs=[VMEM] * 3,
        out_specs=(VMEM,) * 2,
        compiler_params=PARAMS,
        name="blur",
    )(wide, swap(first, rows, 1), swap_later(second, rows))

    table = exchange(adjoint)
    other = swap(table, "shots", 1)
    own, exposure = pick(counts, cells, table, blurred)
    shot_grad = pick_last(counts, cells, other, own)
    return (exposure, shot_grad[None, None, None])


def solution(mesh):
    placed = (
        P("shots", "gy", "gx", None, None),
        P("shots", "gy", "gx", None, None),
        P("shots", "gy", "gx", None),
        P(("shots", "gy"), "gx"),
        P(),
        P(("shots", "gy"), "gx"),
    )
    return jax.shard_map(
        local,
        mesh=mesh,
        in_specs=placed,
        out_specs=(P(("shots", "gy"), "gx"), P("shots", "gy", "gx", None, None)),
        check_vma=False,
    )
```

```python
import functools

import jax
import jax.numpy as jnp
from jax import lax
from jax.experimental import pallas as pl
from jax.experimental.pallas import tpu as pltpu
from jax.sharding import PartitionSpec as P

STEPS = 3
SPAN = 512
CHUNK = 1024
UNROLL = 8
LANES = 128
VMEM = pl.BlockSpec(memory_space=pltpu.VMEM)
HBM = pl.BlockSpec(memory_space=pltpu.HBM)
PARAMS = pltpu.CompilerParams(vmem_limit_bytes=32 << 20)
F32 = jnp.float32
BF16 = jnp.bfloat16


def f32(*shape):
    return jax.ShapeDtypeStruct(shape, F32)


def rows_of(value, kind):
    return jnp.broadcast_to(value, (16, value.shape[1])).astype(kind)


def hot(index, groups, filled):
    width = index.shape[1]
    ids = rows_of(index, jnp.int16)
    iota = lax.broadcasted_iota(jnp.int16, (16, width), 0)
    masks = [ids == iota + jnp.int16(16 * g) for g in range(groups)]
    zero = jnp.bfloat16(0)
    return [jnp.concatenate([jnp.where(m, f, zero) for m in masks], axis=0) for f in filled]


COST = pl.CostEstimate(flops=1 << 30, bytes_accessed=1 << 18, transcendentals=0)


def split(cell):
    return ((cell >> 7) & 3) * 16 + (cell >> 9), cell & 127


def own_core():
    return lax.axis_index("shots") % 2


def alive(counts_ref, strip, k):
    count = jnp.concatenate([counts_ref[pl.ds(strip, 1), :]] * (SPAN // LANES), axis=1)
    return lax.broadcasted_iota(jnp.int32, (1, SPAN), 1) + k < count


def deposit_kernel(side, counts_ref, cells_ref, dose_ref, out_ref):
    core = own_core() ^ side
    slots = cells_ref.shape[1]

    def strip(j, carry):
        o = 2 * j + core
        total = jnp.zeros((2 * 64, LANES), F32)
        for k in range(0, slots, SPAN):
            cell = cells_ref[pl.ds(o, 1), k : k + SPAN]
            dose = jnp.where(alive(counts_ref, o, k), dose_ref[pl.ds(o, 1), k : k + SPAN], 0.0)
            high = dose.astype(BF16).astype(F32)
            chunk, lane = split(cell)
            rows = hot(chunk, 4, [rows_of(high, BF16), rows_of(dose - high, BF16)])
            (cols,) = hot(lane, 8, [jnp.bfloat16(1)])
            total = total + lax.dot_general(
                jnp.concatenate(rows, axis=0),
                cols,
                (((1,), (1,)), ((), ())),
                preferred_element_type=F32,
            )
        both = total[:64] + total[64:]
        for q in range(4):
            out_ref[j, :, q * LANES : (q + 1) * LANES] = both[16 * q : 16 * q + 16]
        return carry

    lax.fori_loop(0, out_ref.shape[0], strip, 0, unroll=UNROLL)


def first_kernel(*refs):
    sources, (out_ref, counts_ref, cells, dose, spread_ref) = refs[:5], refs[5:10]
    counts, materials, coefs, sems = refs[10:]
    targets = (counts, coefs, cells, dose, materials)
    copies = [
        pltpu.make_async_copy(source, target, sems.at[i])
        for i, (source, target) in enumerate(zip(sources, targets))
    ]
    for copy in copies:
        copy.start()
    for copy in copies:
        copy.wait()
    for o in range(counts_ref.shape[0]):
        counts_ref[o : o + 1, :] = jnp.full((1, LANES), counts[o], jnp.int32)
    spread = jnp.zeros(materials.shape, F32)
    for index in range(coefs.shape[0]):
        spread = jnp.where(materials[...] == index, coefs[index], spread)
    spread_ref[...] = spread
    deposit_kernel(1, counts_ref, cells, dose, out_ref)


def deposit_first(counts, coefficients, cells, dose, materials):
    inputs = (counts, coefficients, cells, dose, materials)
    same = lambda value: jax.ShapeDtypeStruct(value.shape, value.dtype)
    return pl.pallas_call(
        first_kernel,
        out_shape=(
            f32(8, 16, 512),
            jax.ShapeDtypeStruct((counts.shape[0], LANES), jnp.int32),
            same(cells),
            same(dose),
            f32(*materials.shape),
        ),
        in_specs=[HBM] * 5,
        out_specs=(VMEM,) * 5,
        scratch_shapes=[
            pltpu.SMEM(counts.shape, jnp.int32),
            pltpu.VMEM(materials.shape, jnp.int32),
            pltpu.SMEM(coefficients.shape, F32),
            pltpu.SemaphoreType.DMA((5,)),
        ],
        compiler_params=PARAMS,
        cost_estimate=COST,
        name="deposit_first",
    )(*(pltpu.with_memory_space_constraint(value, pltpu.HBM) for value in inputs))


def deposit(counts, cells, dose):
    return pl.pallas_call(
        functools.partial(deposit_kernel, 0),
        out_shape=f32(8, 16, 512),
        in_specs=[VMEM] * 3,
        out_specs=VMEM,
        compiler_params=PARAMS,
        cost_estimate=COST,
        name="deposit",
    )(counts, cells, dose)


def gather_kernel(parts_ref, spread_ref, target_ref, mid_ref, first_ref, second_ref):
    strip = parts_ref[0]
    for z in range(1, parts_ref.shape[0]):
        strip = strip + parts_ref[z]
    lane = lax.broadcasted_iota(jnp.int32, (16, LANES), 1)
    left, right = jnp.zeros((16, LANES), F32), jnp.zeros((16, LANES), F32)
    for i, value in enumerate((strip, spread_ref[...], target_ref[...])):
        mid_ref[i] = value
        here = (lane >= 16 * i) & (lane < 16 * i + 8)
        left = jnp.where(here, pltpu.roll(value[:, :LANES], 16 * i, 1), left)
        right = jnp.where(here, pltpu.roll(value[:, -LANES:], 16 * i + 8, 1), right)
    column, columns = lax.axis_index("gx"), lax.axis_size("gx")
    first_ref[...] = jnp.where(column == columns - 1, 0.0, right)
    second_ref[...] = jnp.where(column == 0, 0.0, left)


def widen_kernel(mid_ref, first_ref, second_ref, wide_ref, send_ref, later_ref):
    near = lax.broadcasted_iota(jnp.int32, (16, LANES), 1) < LANES // 2
    left, right = first_ref[...], second_ref[...]
    for i in range(3):
        tile = jnp.where(
            near,
            pltpu.roll(right, (LANES - 16 * i) % LANES, 1),
            pltpu.roll(left, LANES - 8 - 16 * i, 1),
        )
        wide = jnp.concatenate([mid_ref[i], tile], axis=1)
        wide_ref[i] = wide
        if i == 0:
            top, bottom = wide[:8], wide[8:]
        elif i == 1:
            top, bottom = jnp.concatenate([top, wide[:5]]), jnp.concatenate([bottom, wide[11:]])
        else:
            top, bottom = jnp.concatenate([top, wide[:3]]), jnp.concatenate([bottom, wide[13:]])
    line = lax.axis_index("shots") * lax.axis_size("gy") + lax.axis_index("gy")
    last = lax.axis_size("shots") * lax.axis_size("gy") - 1
    send_ref[...] = jnp.where(line == last, 0.0, bottom)
    later_ref[...] = jnp.where(line == 0, 0.0, top)


def neighbours(field):
    height, width = field.shape
    return (
        pltpu.roll(field, 1, 0)
        + pltpu.roll(field, height - 1, 0)
        + pltpu.roll(field, 1, 1)
        + pltpu.roll(field, width - 1, 1)
    )


def blur_kernel(wide_ref, first_ref, second_ref, exposure_ref, adjoint_ref):
    above, below = first_ref[...], second_ref[...]
    width = wide_ref.shape[2]
    blank = lambda rows: jnp.zeros((rows, width), F32)
    field = jnp.concatenate([above[:8], wide_ref[0], below[:8]], axis=0)
    spread = jnp.concatenate(
        [blank(3), above[8:13], wide_ref[1], below[8:13], blank(3)], axis=0
    )
    target = jnp.concatenate(
        [blank(5), above[13:], wide_ref[2], below[13:], blank(5)], axis=0
    )
    for step in range(STEPS):
        field = field + spread * (neighbours(field) - 4.0 * field)
    exposure_ref[...] = field[8:24, :-LANES]
    field = field - target
    for step in range(STEPS):
        weighted = spread * field
        field = field + neighbours(weighted) - 4.0 * weighted
    for q in range(4):
        for z in range(adjoint_ref.shape[0]):
            adjoint_ref[z, 16 * q : 16 * q + 16] = field[8:24, q * LANES : (q + 1) * LANES]


def parts_of(table):
    high = table.astype(BF16)
    return jnp.concatenate([high, (table - high.astype(F32)).astype(BF16)], axis=0)


def pick_span(counts_ref, cells_ref, both, o, k):
    span = pl.ds(k, SPAN)
    chunk, lane = split(cells_ref[pl.ds(o, 1), span])
    (cols,) = hot(lane, 8, [jnp.bfloat16(1)])
    across = jnp.dot(both, cols, preferred_element_type=F32)
    across = across[:64] + across[64:]
    iota = lax.broadcasted_iota(jnp.int32, (8, SPAN), 0)
    chosen = jnp.broadcast_to(chunk, (8, SPAN))
    value = jnp.zeros((8, SPAN), F32)
    for g in range(8):
        value = jnp.where(chosen == iota + 8 * g, across[8 * g : 8 * g + 8], value)
    value = jnp.sum(value, axis=0, keepdims=True)
    return jnp.where(alive(counts_ref, o, k), value, 0.0)


def pick_kernel(counts_ref, cells_ref, table_ref, blurred_ref, own_ref, exposure_hbm, sem):
    copy = pltpu.make_async_copy(blurred_ref, exposure_hbm, sem)
    copy.start()

    def strip(z, carry):
        both = parts_of(table_ref[z])
        for k in range(0, cells_ref.shape[1], SPAN):
            value = pick_span(counts_ref, cells_ref, both, 2 * z + own_core(), k)
            own_ref[pl.ds(z, 1), k : k + SPAN] = value
        return carry

    lax.fori_loop(0, table_ref.shape[0], strip, 0, unroll=UNROLL)
    copy.wait()


def pick(counts, cells, table, blurred):
    return pl.pallas_call(
        pick_kernel,
        out_shape=(f32(table.shape[0], cells.shape[1]), f32(*blurred.shape)),
        in_specs=[VMEM] * 4,
        out_specs=(VMEM, pl.BlockSpec(memory_space=pl.ANY)),
        scratch_shapes=[pltpu.SemaphoreType.DMA],
        compiler_params=PARAMS,
        cost_estimate=COST,
        name="pick",
    )(counts, cells, table, blurred)


def last_kernel(counts_ref, cells_ref, table_ref, own_ref, out_hbm, out_ref, both_ref, sems):
    depth, core = table_ref.shape[0], own_core()
    for z in range(depth):
        out_ref[pl.ds(2 * z + core, 1), :] = own_ref[z : z + 1, :]
        both_ref[z] = parts_of(table_ref[z])

    def copy(i):
        part = pl.ds(pl.multiple_of(i * CHUNK, CHUNK), CHUNK)
        return pltpu.make_async_copy(out_ref.at[:, part], out_hbm.at[:, part], sems.at[i])

    def chunk(i, carry):
        for z in range(depth):
            o = 2 * z + 1 - core
            for j in range(0, CHUNK, SPAN):
                k = pl.multiple_of(i * CHUNK + j, SPAN)
                value = pick_span(counts_ref, cells_ref, both_ref[z], o, k)
                out_ref[pl.ds(o, 1), pl.ds(k, SPAN)] = value
        copy(i).start()
        return carry

    steps = cells_ref.shape[1] // CHUNK
    lax.fori_loop(0, steps, chunk, 0, unroll=True)
    for i in range(steps):
        copy(i).wait()


def pick_last(counts, cells, table, own):
    return pl.pallas_call(
        last_kernel,
        out_shape=f32(*cells.shape),
        in_specs=[VMEM] * 4,
        out_specs=pl.BlockSpec(memory_space=pl.ANY),
        scratch_shapes=[
            pltpu.VMEM(cells.shape, F32),
            pltpu.VMEM((table.shape[0], 2 * 64, LANES), BF16),
            pltpu.SemaphoreType.DMA((cells.shape[1] // CHUNK,)),
        ],
        compiler_params=PARAMS,
        cost_estimate=COST,
        name="pick_last",
    )(counts, cells, table, own)


def swap(value, axes, bits):
    count = lax.axis_size(axes)
    return lax.ppermute(value, axes, [(i, i ^ bits) for i in range(count)])


def shift(value, axes, by):
    count = lax.axis_size(axes)
    return lax.ppermute(value, axes, [(i, (i + by) % count) for i in range(count)])


def local(shot_cells, shot_dose, shot_counts, materials, coefficients, target):
    cells, dose, counts = shot_cells[0, 0, 0], shot_dose[0, 0, 0], shot_counts[0, 0, 0]
    shots = lax.axis_size("shots")
    lines = [[2 * z + c for z in range(shots // 2)] for c in range(2)]

    def exchange(value):
        return lax.all_to_all(value, "shots", 0, 0, axis_index_groups=lines, tiled=True)

    away, counts, cells, dose, spread = deposit_first(
        counts, coefficients, cells, dose, materials
    )
    away = swap(away, "shots", 1)
    parts = exchange(deposit(counts, cells, dose) + away)

    mid, first, second = pl.pallas_call(
        gather_kernel,
        out_shape=(f32(3, 16, 512), f32(16, LANES), f32(16, LANES)),
        in_specs=[VMEM] * 3,
        out_specs=(VMEM,) * 3,
        compiler_params=PARAMS,
        name="gather",
    )(parts, spread, target)
    wide, first, second = pl.pallas_call(
        widen_kernel,
        out_shape=(f32(3, 16, 640), f32(16, 640), f32(16, 640)),
        in_specs=[VMEM] * 3,
        out_specs=(VMEM,) * 3,
        compiler_params=PARAMS,
        name="widen",
    )(mid, shift(first, "gx", 1), shift(second, "gx", -1))
    rows = ("shots", "gy")
    blurred, adjoint = pl.pallas_call(
        blur_kernel,
        out_shape=(f32(16, 512), f32(shots // 2, 64, LANES)),
        in_specs=[VMEM] * 3,
        out_specs=(VMEM,) * 2,
        compiler_params=PARAMS,
        name="blur",
    )(wide, shift(first, rows, 1), shift(second, rows, -1))

    table = exchange(adjoint)
    other = swap(table, "shots", 1)
    own, exposure = pick(counts, cells, table, blurred)
    shot_grad = pick_last(counts, cells, other, own)
    return (exposure, shot_grad[None, None, None])


def solution(mesh):
    placed = (
        P("shots", "gy", "gx", None, None),
        P("shots", "gy", "gx", None, None),
        P("shots", "gy", "gx", None),
        P(("shots", "gy"), "gx"),
        P(),
        P(("shots", "gy"), "gx"),
    )
    return jax.shard_map(
        local,
        mesh=mesh,
        in_specs=placed,
        out_specs=(P(("shots", "gy"), "gx"), P("shots", "gy", "gx", None, None)),
        check_vma=False,
    )
```

```python
import functools

import jax
import jax.numpy as jnp
from jax import lax
from jax.experimental import pallas as pl
from jax.experimental.pallas import tpu as pltpu
from jax.sharding import PartitionSpec as P

STEPS = 3
SPAN = 512
CHUNK = 1024
UNROLL = 8
LANES = 128
VMEM = pl.BlockSpec(memory_space=pltpu.VMEM)
HBM = pl.BlockSpec(memory_space=pltpu.HBM)
PARAMS = pltpu.CompilerParams(vmem_limit_bytes=32 << 20)
F32 = jnp.float32
BF16 = jnp.bfloat16


def f32(*shape):
    return jax.ShapeDtypeStruct(shape, F32)


def rows_of(value, kind):
    return jnp.broadcast_to(value, (16, value.shape[1])).astype(kind)


def hot(index, groups, filled):
    width = index.shape[1]
    ids = rows_of(index, jnp.int16)
    iota = lax.broadcasted_iota(jnp.int16, (16, width), 0)
    masks = [ids == iota + jnp.int16(16 * g) for g in range(groups)]
    zero = jnp.bfloat16(0)
    return [jnp.concatenate([jnp.where(m, f, zero) for m in masks], axis=0) for f in filled]


COST = pl.CostEstimate(flops=1 << 30, bytes_accessed=1 << 18, transcendentals=0)


def split(cell):
    return ((cell >> 7) & 3) * 16 + (cell >> 9), cell & 127


def own_core():
    return lax.axis_index("shots") % 2


def alive(counts_ref, strip, k):
    count = jnp.concatenate([counts_ref[pl.ds(strip, 1), :]] * (SPAN // LANES), axis=1)
    return lax.broadcasted_iota(jnp.int32, (1, SPAN), 1) + k < count


def deposit_kernel(side, counts_ref, cells_ref, dose_ref, out_ref):
    core = own_core() ^ side
    slots = cells_ref.shape[1]

    def strip(j, carry):
        o = 2 * j + core
        total = jnp.zeros((2 * 64, LANES), F32)
        for k in range(0, slots, SPAN):
            cell = cells_ref[pl.ds(o, 1), k : k + SPAN]
            dose = jnp.where(alive(counts_ref, o, k), dose_ref[pl.ds(o, 1), k : k + SPAN], 0.0)
            high = dose.astype(BF16).astype(F32)
            chunk, lane = split(cell)
            rows = hot(chunk, 4, [rows_of(high, BF16), rows_of(dose - high, BF16)])
            (cols,) = hot(lane, 8, [jnp.bfloat16(1)])
            total = total + lax.dot_general(
                jnp.concatenate(rows, axis=0),
                cols,
                (((1,), (1,)), ((), ())),
                preferred_element_type=F32,
            )
        both = total[:64] + total[64:]
        for q in range(4):
            out_ref[j, :, q * LANES : (q + 1) * LANES] = both[16 * q : 16 * q + 16]
        return carry

    lax.fori_loop(0, out_ref.shape[0], strip, 0, unroll=UNROLL)


def first_kernel(*refs):
    sources, (out_ref, counts_ref, cells, dose, spread_ref) = refs[:5], refs[5:10]
    counts, materials, coefs, sems = refs[10:]
    targets = (counts, coefs, cells, dose, materials)
    copies = [
        pltpu.make_async_copy(source, target, sems.at[i])
        for i, (source, target) in enumerate(zip(sources, targets))
    ]
    for copy in copies:
        copy.start()
    for copy in copies:
        copy.wait()
    for o in range(counts_ref.shape[0]):
        counts_ref[o : o + 1, :] = jnp.full((1, LANES), counts[o], jnp.int32)
    spread = jnp.zeros(materials.shape, F32)
    for index in range(coefs.shape[0]):
        spread = jnp.where(materials[...] == index, coefs[index], spread)
    spread_ref[...] = spread
    deposit_kernel(1, counts_ref, cells, dose, out_ref)


def deposit_first(counts, coefficients, cells, dose, materials):
    inputs = (counts, coefficients, cells, dose, materials)
    same = lambda value: jax.ShapeDtypeStruct(value.shape, value.dtype)
    return pl.pallas_call(
        first_kernel,
        out_shape=(
            f32(8, 16, 512),
            jax.ShapeDtypeStruct((counts.shape[0], LANES), jnp.int32),
            same(cells),
            same(dose),
            f32(*materials.shape),
        ),
        in_specs=[HBM] * 5,
        out_specs=(VMEM,) * 5,
        scratch_shapes=[
            pltpu.SMEM(counts.shape, jnp.int32),
            pltpu.VMEM(materials.shape, jnp.int32),
            pltpu.SMEM(coefficients.shape, F32),
            pltpu.SemaphoreType.DMA((5,)),
        ],
        compiler_params=PARAMS,
        cost_estimate=COST,
        name="deposit_first",
    )(*(pltpu.with_memory_space_constraint(value, pltpu.HBM) for value in inputs))


def deposit(counts, cells, dose):
    return pl.pallas_call(
        functools.partial(deposit_kernel, 0),
        out_shape=f32(8, 16, 512),
        in_specs=[VMEM] * 3,
        out_specs=VMEM,
        compiler_params=PARAMS,
        cost_estimate=COST,
        name="deposit",
    )(counts, cells, dose)


def gather_kernel(parts_ref, spread_ref, target_ref, mid_ref, down_ref, up_ref):
    strip = parts_ref[0]
    for z in range(1, parts_ref.shape[0]):
        strip = strip + parts_ref[z]
    spread, target = spread_ref[...], target_ref[...]
    for i, value in enumerate((strip, spread, target)):
        mid_ref[i] = value
    line = lax.axis_index("shots") * lax.axis_size("gy") + lax.axis_index("gy")
    last = lax.axis_size("shots") * lax.axis_size("gy") - 1
    bottom = jnp.concatenate([strip[8:], spread[11:], target[13:]], axis=0)
    top = jnp.concatenate([strip[:8], spread[:5], target[:3]], axis=0)
    down_ref[...] = jnp.where(line == last, 0.0, bottom)
    up_ref[...] = jnp.where(line == 0, 0.0, top)


def heighten_kernel(mid_ref, above_ref, below_ref, tall_ref, right_ref, left_ref):
    above, below = above_ref[...], below_ref[...]
    blank = lambda rows: jnp.zeros((rows, above.shape[1]), F32)
    fields = (
        [above[:8], mid_ref[0], below[:8]],
        [blank(3), above[8:13], mid_ref[1], below[8:13], blank(3)],
        [blank(5), above[13:], mid_ref[2], below[13:], blank(5)],
    )
    lane = lax.broadcasted_iota(jnp.int32, (32, LANES), 1)
    left, right = jnp.zeros((32, LANES), F32), jnp.zeros((32, LANES), F32)
    for i, pieces in enumerate(fields):
        value = jnp.concatenate(pieces, axis=0)
        tall_ref[i] = value
        here = (lane >= 16 * i) & (lane < 16 * i + 8)
        left = jnp.where(here, pltpu.roll(value[:, :LANES], 16 * i, 1), left)
        right = jnp.where(here, pltpu.roll(value[:, -LANES:], 16 * i + 8, 1), right)
    column, columns = lax.axis_index("gx"), lax.axis_size("gx")
    right_ref[...] = jnp.where(column == columns - 1, 0.0, right)
    left_ref[...] = jnp.where(column == 0, 0.0, left)


def neighbours(field):
    height, width = field.shape
    return (
        pltpu.roll(field, 1, 0)
        + pltpu.roll(field, height - 1, 0)
        + pltpu.roll(field, 1, 1)
        + pltpu.roll(field, width - 1, 1)
    )


def blur_kernel(tall_ref, left_ref, right_ref, exposure_ref, adjoint_ref):
    left, right = left_ref[...], right_ref[...]
    near = lax.broadcasted_iota(jnp.int32, (32, LANES), 1) < LANES // 2
    fields = []
    for i in range(3):
        tile = jnp.where(
            near,
            pltpu.roll(right, (LANES - 16 * i) % LANES, 1),
            pltpu.roll(left, LANES - 8 - 16 * i, 1),
        )
        fields.append(jnp.concatenate([tall_ref[i], tile], axis=1))
    field, spread, target = fields
    for step in range(STEPS):
        field = field + spread * (neighbours(field) - 4.0 * field)
    exposure_ref[...] = field[8:24, :-LANES]
    field = field - target
    for step in range(STEPS):
        weighted = spread * field
        field = field + neighbours(weighted) - 4.0 * weighted
    for q in range(4):
        for z in range(adjoint_ref.shape[0]):
            adjoint_ref[z, 16 * q : 16 * q + 16] = field[8:24, q * LANES : (q + 1) * LANES]


def parts_of(table):
    high = table.astype(BF16)
    return jnp.concatenate([high, (table - high.astype(F32)).astype(BF16)], axis=0)


def pick_span(counts_ref, cells_ref, both, o, k):
    span = pl.ds(k, SPAN)
    chunk, lane = split(cells_ref[pl.ds(o, 1), span])
    (cols,) = hot(lane, 8, [jnp.bfloat16(1)])
    across = jnp.dot(both, cols, preferred_element_type=F32)
    across = across[:64] + across[64:]
    iota = lax.broadcasted_iota(jnp.int32, (8, SPAN), 0)
    chosen = jnp.broadcast_to(chunk, (8, SPAN))
    value = jnp.zeros((8, SPAN), F32)
    for g in range(8):
        value = jnp.where(chosen == iota + 8 * g, across[8 * g : 8 * g + 8], value)
    value = jnp.sum(value, axis=0, keepdims=True)
    return jnp.where(alive(counts_ref, o, k), value, 0.0)


def pick_kernel(counts_ref, cells_ref, table_ref, blurred_ref, own_ref, exposure_hbm, sem):
    copy = pltpu.make_async_copy(blurred_ref, exposure_hbm, sem)
    copy.start()

    def strip(z, carry):
        both = parts_of(table_ref[z])
        for k in range(0, cells_ref.shape[1], SPAN):
            value = pick_span(counts_ref, cells_ref, both, 2 * z + own_core(), k)
            own_ref[pl.ds(z, 1), k : k + SPAN] = value
        return carry

    lax.fori_loop(0, table_ref.shape[0], strip, 0, unroll=UNROLL)
    copy.wait()


def pick(counts, cells, table, blurred):
    return pl.pallas_call(
        pick_kernel,
        out_shape=(f32(table.shape[0], cells.shape[1]), f32(*blurred.shape)),
        in_specs=[VMEM] * 4,
        out_specs=(VMEM, pl.BlockSpec(memory_space=pl.ANY)),
        scratch_shapes=[pltpu.SemaphoreType.DMA],
        compiler_params=PARAMS,
        cost_estimate=COST,
        name="pick",
    )(counts, cells, table, blurred)


def last_kernel(counts_ref, cells_ref, table_ref, own_ref, out_hbm, out_ref, both_ref, sems):
    depth, core = table_ref.shape[0], own_core()
    for z in range(depth):
        out_ref[pl.ds(2 * z + core, 1), :] = own_ref[z : z + 1, :]
        both_ref[z] = parts_of(table_ref[z])

    def copy(i):
        part = pl.ds(pl.multiple_of(i * CHUNK, CHUNK), CHUNK)
        return pltpu.make_async_copy(out_ref.at[:, part], out_hbm.at[:, part], sems.at[i])

    def chunk(i, carry):
        for z in range(depth):
            o = 2 * z + 1 - core
            for j in range(0, CHUNK, SPAN):
                k = pl.multiple_of(i * CHUNK + j, SPAN)
                value = pick_span(counts_ref, cells_ref, both_ref[z], o, k)
                out_ref[pl.ds(o, 1), pl.ds(k, SPAN)] = value
        copy(i).start()
        return carry

    steps = cells_ref.shape[1] // CHUNK
    lax.fori_loop(0, steps, chunk, 0, unroll=True)
    for i in range(steps):
        copy(i).wait()


def pick_last(counts, cells, table, own):
    return pl.pallas_call(
        last_kernel,
        out_shape=f32(*cells.shape),
        in_specs=[VMEM] * 4,
        out_specs=pl.BlockSpec(memory_space=pl.ANY),
        scratch_shapes=[
            pltpu.VMEM(cells.shape, F32),
            pltpu.VMEM((table.shape[0], 2 * 64, LANES), BF16),
            pltpu.SemaphoreType.DMA((cells.shape[1] // CHUNK,)),
        ],
        compiler_params=PARAMS,
        cost_estimate=COST,
        name="pick_last",
    )(counts, cells, table, own)


def swap(value, axes, bits):
    count = lax.axis_size(axes)
    return lax.ppermute(value, axes, [(i, i ^ bits) for i in range(count)])


def shift(value, axes, by):
    count = lax.axis_size(axes)
    return lax.ppermute(value, axes, [(i, (i + by) % count) for i in range(count)])


def local(shot_cells, shot_dose, shot_counts, materials, coefficients, target):
    cells, dose, counts = shot_cells[0, 0, 0], shot_dose[0, 0, 0], shot_counts[0, 0, 0]
    shots = lax.axis_size("shots")
    lines = [[2 * z + c for z in range(shots // 2)] for c in range(2)]

    def exchange(value):
        return lax.all_to_all(value, "shots", 0, 0, axis_index_groups=lines, tiled=True)

    away, counts, cells, dose, spread = deposit_first(
        counts, coefficients, cells, dose, materials
    )
    away = swap(away, "shots", 1)
    parts = exchange(deposit(counts, cells, dose) + away)

    row, edge = f32(16, 512), f32(32, LANES)
    mid, down, up = pl.pallas_call(
        gather_kernel,
        out_shape=(f32(3, 16, 512), row, row),
        in_specs=[VMEM] * 3,
        out_specs=(VMEM,) * 3,
        compiler_params=PARAMS,
        name="gather",
    )(parts, spread, target)
    rows = ("shots", "gy")
    tall, right, left = pl.pallas_call(
        heighten_kernel,
        out_shape=(f32(3, 32, 512), edge, edge),
        in_specs=[VMEM] * 3,
        out_specs=(VMEM,) * 3,
        compiler_params=PARAMS,
        name="heighten",
    )(mid, shift(down, rows, 1), shift(up, rows, -1))
    blurred, adjoint = pl.pallas_call(
        blur_kernel,
        out_shape=(f32(16, 512), f32(shots // 2, 64, LANES)),
        in_specs=[VMEM] * 3,
        out_specs=(VMEM,) * 2,
        compiler_params=PARAMS,
        name="blur",
    )(tall, shift(right, "gx", 1), shift(left, "gx", -1))

    table = exchange(adjoint)
    other = swap(table, "shots", 1)
    own, exposure = pick(counts, cells, table, blurred)
    shot_grad = pick_last(counts, cells, other, own)
    return (exposure, shot_grad[None, None, None])


def solution(mesh):
    placed = (
        P("shots", "gy", "gx", None, None),
        P("shots", "gy", "gx", None, None),
        P("shots", "gy", "gx", None),
        P(("shots", "gy"), "gx"),
        P(),
        P(("shots", "gy"), "gx"),
    )
    return jax.shard_map(
        local,
        mesh=mesh,
        in_specs=placed,
        out_specs=(P(("shots", "gy"), "gx"), P("shots", "gy", "gx", None, None)),
        check_vma=False,
    )
```
